32 devices in a mesh: dp: 4 (over y, core), mp: 8 (over z, x).
Axes of the slice: x: 2, y: 2, z: 4, core: 2. Of those that a mesh axis runs over, the one named last changes fastest.
Arguments:
- acts: bfloat16 [512, 8192], P('mp', 'dp'), may hold values from -6 to 6
- grads: bfloat16 [512, 28672], P('dp', 'mp'), may hold values from -6 to 6
- query_acts: bfloat16 [256, 8192], P('mp', 'dp'), may hold values from -6 to 6
- query_grads: bfloat16 [256, 28672], P('dp', 'mp'), may hold values from -6 to 6
- basis_in: bfloat16 [8192, 8192], P('dp', 'mp'), may hold values from -0.0625 to 0.0625
- basis_out: bfloat16 [28672, 14336], P('mp', 'dp'), may hold values from -0.03125 to 0.03125
Outputs:
- eigenvalues: float32 [8192, 14336], P('mp', 'dp')
- scores: float32 [16, 512], replicated
The draws below stay inside these ranges and needn't reach their ends.
All inputs are finite; a program needn't handle non-finite values.
Results may differ from the reference program's by a relative error of at most 0.0047.
Values may be sent and summed in bfloat16 or wider, within the bound.
A program may use at most 128 MiB of HBM per device.

```python
import math
import jax
import jax.numpy as jnp
from jax import lax

D = 8192
FF = 28672
K = 14336
TOKENS = 512
NQ = 16
QTOK = 16


def block_scale(rng, dims, split, least, top_value):
    loudness, own = 1.0, jax.random.fold_in(rng, 6)
    for position, parts in split:
        draws = jnp.exp(jax.random.uniform(jax.random.fold_in(own, position), (parts,), jnp.float32, least / len(split), top_value / len(split)))
        loudness = loudness * jnp.repeat(draws, dims[position] // parts).reshape([-1 if axis == position else 1 for axis in range(len(dims))])
    return loudness


def noise(own_key, dims, scale, reach, pieces=(), kind=jnp.bfloat16):
    values = jax.random.normal(own_key, dims, jnp.float32) * scale
    if len(pieces) > 0:
        values = block_scale(own_key, dims, pieces, -0.22, 0.18) * values
    return jnp.clip(values, min=-reach, max=reach).astype(kind)


def setup_inputs(seed: int = 0) -> dict:
    key_list = jax.random.split(jax.random.key(seed), 7)
    return {
        "acts": noise(key_list[0], (TOKENS, D), 1.0, 6.0, ((0, 8), (1, 4))),
        "grads": noise(key_list[1], (TOKENS, FF), 1.0, 6.0, ((0, 4), (1, 8))),
        "query_acts": noise(key_list[2], (NQ * QTOK, D), 1.0, 6.0, ((0, 8), (1, 4))),
        "query_grads": noise(key_list[3], (NQ * QTOK, FF), 1.0, 6.0, ((0, 4), (1, 8))),
        "basis_in": noise(key_list[4], (D, D), D ** -0.5, 0.0625, ((0, 4), (1, 8))),
        "basis_out": noise(key_list[5], (FF, K), FF ** -0.5, 0.03125, ((0, 8), (1, 4))),
    }


def reference(acts, grads, query_acts, query_grads, basis_in, basis_out):
    rot_acts = jnp.dot(acts, basis_in, preferred_element_type=jnp.float32).astype(jnp.bfloat16)
    rot_grads = jnp.dot(grads, basis_out, preferred_element_type=jnp.float32).astype(jnp.bfloat16)
    rot_qacts = jnp.dot(query_acts, basis_in, preferred_element_type=jnp.float32).astype(jnp.bfloat16)
    rot_qgrads = jnp.dot(query_grads, basis_out, preferred_element_type=jnp.float32).astype(jnp.bfloat16)
    sq_acts = (rot_acts.astype(jnp.float32) ** 2).astype(jnp.bfloat16)
    sq_grads = (rot_grads.astype(jnp.float32) ** 2).astype(jnp.bfloat16)
    count = acts.shape[0]
    eigenvalues = jnp.dot(sq_acts.T, sq_grads, preferred_element_type=jnp.float32) / count
    queries = query_acts.shape[0] // QTOK
    qa_blocks = rot_qacts.reshape(queries, QTOK, rot_qacts.shape[1])
    qg_blocks = rot_qgrads.reshape(queries, QTOK, rot_qgrads.shape[1])

    def one_query(pair):
        left, right = pair
        rotated = jnp.dot(left.T, right, preferred_element_type=jnp.float32) / QTOK
        precond = (rotated / (eigenvalues + 0.1)).astype(jnp.bfloat16)
        mapped = jnp.dot(rot_acts, precond, preferred_element_type=jnp.float32)
        return lax.optimization_barrier(jnp.sum(mapped * rot_grads.astype(jnp.float32), axis=1))
    scores = lax.map(one_query, (qa_blocks, qg_blocks)) * math.sqrt(QTOK / (D * K))
    return (eigenvalues, scores)
```

```python
import functools
import math

import jax
import jax.numpy as jnp
from jax import lax
from jax.experimental import pallas as pl
from jax.experimental.pallas import tpu as pltpu
from jax.sharding import PartitionSpec as P

QTOK = 16
F32 = jnp.float32
BF16 = jnp.bfloat16
MESH = pl.DeviceIdType.MESH


def bit(v, b):
    return (v // 2**b) % 2


def reverse_bits(v, k):
    return sum(bit(v, b) * 2 ** (k - 1 - b) for b in range(k))


def log2(n):
    return n.bit_length() - 1


def kernel(cfg, *refs):
    n_mp, n_dp, chunks = cfg
    k_mp, k_dp = log2(n_mp), log2(n_dp)
    (
        acts, q_acts, grads, q_grads, basis_in, basis_out, eig_out, scores_out,
        gin, gout, bin_v, bout_v, acc, send_rs, recv_rs, rot_out, acc_in, recv_in, rot_in,
        act_t, sq_act_t, qact_t, grad_t, sq_grad, qgrad, inverse, eig_v, part, part_in,
        load_sem, bout_sem, eig_sem, gin_s, gin_r, gout_s, gout_r,
        rs_s, rs_r, ag_s, ag_r, irs_s, irs_r, iag_s, iag_r, ps_s, ps_r,
    ) = refs
    dp, mp = lax.axis_index("dp"), lax.axis_index("mp")
    pos_m, pos_d = reverse_bits(mp, k_mp), reverse_bits(dp, k_dp)
    tok_m, qry_m = acts.shape[0], q_acts.shape[0]
    tok_d, qry_d = grads.shape[0], q_grads.shape[0]
    row_m, row_d = tok_m + qry_m, tok_d + qry_d
    rows = row_m * n_mp
    tokens, queries = tok_m * n_mp, qry_m * n_mp // QTOK
    width_i = basis_in.shape[1]
    cw = basis_out.shape[1] // chunks
    ti = 256

    def along_mp(b):
        return (dp, mp + (1 - 2 * bit(mp, b)) * 2**b)

    def along_dp(b):
        return (dp + (1 - 2 * bit(dp, b)) * 2**b, mp)

    def remote(src, dst, s, r, to):
        return pltpu.make_async_remote_copy(
            src_ref=src, dst_ref=dst, send_sem=s, recv_sem=r, device_id=to, device_id_type=MESH
        )

    def rows_at(start, size):
        return pl.ds(pl.multiple_of(start, 16), size)

    def split_start(me, k, step):
        size = rows // 2**step
        return sum(bit(me, b) * (rows // 2 ** (b + 1)) for b in range(step)), size

    barrier = pltpu.get_barrier_semaphore()
    for b in range(k_mp):
        pl.semaphore_signal(barrier, inc=1, device_id=along_mp(b), device_id_type=MESH)
    for b in range(k_dp):
        pl.semaphore_signal(barrier, inc=1, device_id=along_dp(b), device_id_type=MESH)

    def load_chunk(c):
        columns = pl.ds(pl.multiple_of(c * cw, 128), cw)
        return pltpu.make_async_copy(
            basis_out.at[:, columns], bout_v.at[lax.rem(c, 2)], bout_sem.at[c]
        )

    loads = [
        pltpu.make_async_copy(grads, gout.at[rows_at(pos_d * row_d, tok_d)], load_sem.at[0]),
        pltpu.make_async_copy(
            q_grads, gout.at[rows_at(pos_d * row_d + tok_d, qry_d)], load_sem.at[1]
        ),
        pltpu.make_async_copy(acts, gin.at[rows_at(pos_m * row_m, tok_m)], load_sem.at[2]),
        pltpu.make_async_copy(
            q_acts, gin.at[rows_at(pos_m * row_m + tok_m, qry_m)], load_sem.at[3]
        ),
    ]
    load_bin = pltpu.make_async_copy(basis_in, bin_v, load_sem.at[4])
    for copy in loads:
        copy.start()
    load_chunk(0).start()
    load_chunk(1).start()
    load_bin.start()
    pl.semaphore_wait(barrier, k_mp + k_dp)

    def gather_step(buf, me, pos, k, per, step, s, r, along):
        block = rows_at((pos // 2**step) * 2**step * per, per * 2**step)
        return remote(buf.at[block], buf.at[block], s.at[step], r.at[step], along(k - 1 - step))

    gin_steps = [
        gather_step(gin, mp, pos_m, k_mp, row_m, s, gin_s, gin_r, along_mp) for s in range(k_mp)
    ]
    gout_steps = [
        gather_step(gout, dp, pos_d, k_dp, row_d, s, gout_s, gout_r, along_dp) for s in range(k_dp)
    ]
    loads[0].wait()
    loads[1].wait()
    gout_steps[0].start()
    loads[2].wait()
    loads[3].wait()
    gin_steps[0].start()
    for s in range(1, k_mp):
        gin_steps[s - 1].wait_recv()
        gin_steps[s].start()
    for s in range(1, k_dp):
        gout_steps[s - 1].wait_recv()
        gout_steps[s].start()
    gout_steps[k_dp - 1].wait_recv()
    part[0] = jnp.zeros_like(part[0])

    rs_at, offset = [], 0
    for s in range(k_mp):
        rs_at.append(offset)
        offset += rows // 2 ** (s + 1)
    irs_at, offset = [], 0
    for s in range(k_dp):
        irs_at.append(offset)
        offset += rows // 2 ** (s + 1)

    def rs_copy(s, c):
        size = rows // 2 ** (s + 1)
        slot = pl.ds(rs_at[s], size)
        return remote(
            send_rs.at[c, slot], recv_rs.at[c, slot], rs_s.at[s, c], rs_r.at[s, c], along_mp(s)
        )

    def ag_copy(s, c):
        start, size = split_start(mp, k_mp, k_mp - s)
        block = rows_at(start, size)
        return remote(
            rot_out.at[c, block], rot_out.at[c, block], ag_s.at[s, c], ag_r.at[s, c],
            along_mp(k_mp - 1 - s),
        )

    def irs_copy(s):
        start, size = split_start(dp, k_dp, s)
        half = size // 2
        src = rows_at(start + (1 - bit(dp, s)) * half, half)
        return remote(
            acc_in.at[src], recv_in.at[pl.ds(irs_at[s], half)], irs_s.at[s], irs_r.at[s], along_dp(s)
        )

    def iag_copy(s):
        start, size = split_start(dp, k_dp, k_dp - s)
        block = rows_at(start, size)
        return remote(
            rot_in.at[block], rot_in.at[block], iag_s.at[s], iag_r.at[s], along_dp(k_dp - 1 - s)
        )

    half = rows // 2

    def rotate_out(c):
        load_chunk(c).wait()
        slot, ring = lax.rem(c, 2), lax.rem(c, k_mp + 1)
        theirs = rows_at((1 - bit(mp, 0)) * half, half)
        mine = rows_at(bit(mp, 0) * half, half)
        tile = 256

        @pl.loop(0, cw // tile)
        def _(j):
            columns = pl.ds(pl.multiple_of(j * tile, tile), tile)
            out = jnp.dot(gout[theirs, :], bout_v[slot, :, columns], preferred_element_type=F32)
            send_rs[c, pl.ds(0, half), columns] = out.astype(BF16)

        rs_copy(0, c).start()

        @pl.loop(0, cw // tile)
        def _(j):
            columns = pl.ds(pl.multiple_of(j * tile, tile), tile)
            acc[ring, :, columns] = jnp.dot(
                gout[mine, :], bout_v[slot, :, columns], preferred_element_type=F32
            )

        @pl.when(c + 2 < chunks)
        def _():
            load_chunk(c + 2).start()

    def reduce_out(s, c):
        rs_copy(s - 1, c).wait_recv()
        ring = lax.rem(c, k_mp + 1)
        start, size = split_start(mp, k_mp, s)
        start = start - bit(mp, 0) * half
        if s == k_mp:
            total = acc[ring, rows_at(start, size), :] + recv_rs[
                c, pl.ds(rs_at[s - 1], size), :
            ].astype(F32)
            begin, _ = split_start(mp, k_mp, k_mp)
            rot_out[c, rows_at(begin, size), :] = total.astype(BF16)
            ag_copy(0, c).start()
            return
        part_size = size // 2
        theirs, mine = (1 - bit(mp, s)) * part_size, bit(mp, s) * part_size
        base = rs_at[s - 1]
        send_rs[c, pl.ds(rs_at[s], part_size), :] = (
            acc[ring, rows_at(start + theirs, part_size), :]
            + recv_rs[c, rows_at(base + theirs, part_size), :].astype(F32)
        ).astype(BF16)
        rs_copy(s, c).start()
        acc[ring, rows_at(start + mine, part_size), :] = acc[
            ring, rows_at(start + mine, part_size), :
        ] + recv_rs[c, rows_at(base + mine, part_size), :].astype(F32)

    def spread_out(s, c):
        ag_copy(s - 1, c).wait_recv()
        if s < k_mp:
            ag_copy(s, c).start()

    def rotate_in():
        gin_steps[k_mp - 1].wait_recv()
        load_bin.wait()

        @pl.loop(0, width_i // ti)
        def _(j):
            columns = pl.ds(pl.multiple_of(j * ti, ti), ti)
            acc_in[:, columns] = jnp.dot(
                gin[...], bin_v[:, columns], preferred_element_type=F32
            )

        irs_copy(0).start()

    def reduce_in(s):
        irs_copy(s - 1).wait_recv()
        start, size = split_start(dp, k_dp, s)
        where = rows_at(start, size)
        total = acc_in[where, :] + recv_in[pl.ds(irs_at[s - 1], size), :]
        if s == k_dp:
            rot_in[where, :] = total.astype(BF16)
            iag_copy(0).start()
        else:
            acc_in[where, :] = total
            irs_copy(s).start()

    def spread_in(s):
        iag_copy(s - 1).wait_recv()
        if s < k_dp:
            iag_copy(s).start()
            return
        order = [reverse_bits(m, k_mp) * row_m for m in range(n_mp)]
        for i in range(width_i // ti):
            cols = pl.ds(i * ti, ti)
            tok = jnp.concatenate([rot_in[pl.ds(p, tok_m), cols] for p in order], axis=0)
            qry = jnp.concatenate([rot_in[pl.ds(p + tok_m, qry_m), cols] for p in order], axis=0)
            flipped = tok.astype(F32).T
            act_t[cols, :] = flipped
            sq_act_t[cols, :] = (flipped * flipped).astype(BF16)
            qact_t[cols, :] = qry.astype(F32).T.astype(BF16)

    def eig_copy(c):
        columns = pl.ds(pl.multiple_of(c * cw, 128), cw)
        return pltpu.make_async_copy(
            eig_v.at[lax.rem(c, 2)], eig_out.at[:, columns], eig_sem.at[c]
        )

    def score(c):
        @pl.when(c >= 2)
        def _():
            eig_copy(c - 2).wait()

        order = [reverse_bits(d, k_dp) * row_d for d in range(n_dp)]
        for j in range(cw // ti):
            cols = pl.ds(j * ti, ti)
            tok = jnp.concatenate([rot_out[c, pl.ds(p, tok_d), cols] for p in order], axis=0)
            wide = tok.astype(F32)
            grad_t[cols, :] = wide.T.astype(BF16)
            sq_grad[:, cols] = (wide * wide).astype(BF16)
        for d, p in enumerate(order):
            qgrad[pl.ds(d * qry_d, qry_d), :] = rot_out[c, pl.ds(p + tok_d, qry_d), :]
        slot = lax.rem(c, 2)

        @pl.loop(0, width_i // ti)
        def _(i):
            at = pl.ds(pl.multiple_of(i * ti, ti), ti)
            eig = jnp.dot(sq_act_t[at, :], sq_grad[...], preferred_element_type=F32) * (
                1.0 / tokens
            )
            eig_v[slot, at, :] = eig
            inverse[at, :] = (1.0 / QTOK) / (eig + 0.1)

        eig_copy(c).start()

        @pl.loop(0, queries)
        def _(q):
            owner = lax.broadcasted_iota(jnp.int32, qgrad.shape, 0) // QTOK
            right = jnp.where(owner == q, qgrad[...].astype(F32), 0.0).astype(BF16)
            total = jnp.zeros((1, tokens), F32)
            for i in range(width_i // ti):
                at = pl.ds(i * ti, ti)
                rotated = jnp.dot(qact_t[at, :], right, preferred_element_type=F32)
                precond = (rotated * inverse[at, :]).astype(BF16)
                mapped = jnp.dot(precond, grad_t[...], preferred_element_type=F32)
                total = total + jnp.sum(mapped * act_t[at, :], axis=0, keepdims=True)
            part[0, pl.ds(q, 1), :] = part[0, pl.ds(q, 1), :] + total

    lag = 2 * k_mp

    @pl.loop(0, chunks + lag)
    def _(w):
        @pl.when(w < chunks)
        def _():
            rotate_out(w)

        def staged(s, run):
            @pl.when(jnp.logical_and(w >= s, w < chunks + s))
            def _():
                run(w - s)

        for s in range(1, k_mp + 1):
            staged(s, functools.partial(reduce_out, s))
        for s in range(1, k_mp):
            staged(k_mp + s, functools.partial(spread_out, s))

        in_stages = (
            [rotate_in]
            + [functools.partial(reduce_in, s) for s in range(1, k_dp + 1)]
            + [functools.partial(spread_in, s) for s in range(1, k_dp + 1)]
        )
        for n, run in enumerate(in_stages):
            pl.when(w == n + 1)(run)

        staged(lag, functools.partial(spread_out, k_mp))
        staged(lag, score)

    partners = [along_dp(b) for b in range(k_dp)] + [along_mp(b) for b in range(k_mp)]
    for n, to in enumerate(partners):
        copy = remote(part.at[n], part_in.at[n], ps_s.at[n], ps_r.at[n], to)
        copy.start()
        copy.wait_recv()
        part[n + 1] = part[n] + part_in[n]
        copy.wait_send()
    scale = math.sqrt(QTOK / (width_i * n_mp * basis_out.shape[1] * n_dp))
    scores_out[...] = part[len(partners)] * scale

    for copy in gin_steps + gout_steps:
        copy.wait_send()
    for s in range(k_dp):
        irs_copy(s).wait_send()
        iag_copy(s).wait_send()

    @pl.loop(0, chunks)
    def _(c):
        for s in range(k_mp):
            rs_copy(s, c).wait_send()
            ag_copy(s, c).wait_send()

    eig_copy(jnp.int32(chunks - 2)).wait()
    eig_copy(jnp.int32(chunks - 1)).wait()


def fused(n_mp, n_dp, chunks, acts, grads, query_acts, query_grads, basis_in, basis_out):
    k_mp, k_dp = log2(n_mp), log2(n_dp)
    rows = (acts.shape[0] + query_acts.shape[0]) * n_mp
    tokens = acts.shape[0] * n_mp
    queries = query_acts.shape[0] * n_mp
    depth_in, width_i = basis_in.shape
    depth_out, width_o = basis_out.shape
    cw = width_o // chunks
    moved = rows - rows // n_mp
    moved_in = rows - rows // n_dp
    hops = k_mp + k_dp
    small = (hops, queries // QTOK, tokens)
    dma = pltpu.SemaphoreType.DMA
    scratch = [
        pltpu.VMEM((rows, depth_in), BF16),
        pltpu.VMEM((rows, depth_out), BF16),
        pltpu.VMEM((depth_in, width_i), BF16),
        pltpu.VMEM((2, depth_out, cw), BF16),
        pltpu.VMEM((k_mp + 1, rows // 2, cw), F32),
        pltpu.VMEM((chunks, moved, cw), BF16),
        pltpu.VMEM((chunks, moved, cw), BF16),
        pltpu.VMEM((chunks, rows, cw), BF16),
        pltpu.VMEM((rows, width_i), F32),
        pltpu.VMEM((moved_in, width_i), F32),
        pltpu.VMEM((rows, width_i), BF16),
        pltpu.VMEM((width_i, tokens), F32),
        pltpu.VMEM((width_i, tokens), BF16),
        pltpu.VMEM((width_i, queries), BF16),
        pltpu.VMEM((cw, tokens), BF16),
        pltpu.VMEM((tokens, cw), BF16),
        pltpu.VMEM((queries, cw), BF16),
        pltpu.VMEM((width_i, cw), F32),
        pltpu.VMEM((2, width_i, cw), F32),
        pltpu.VMEM((hops + 1,) + small[1:], F32),
        pltpu.VMEM(small, F32),
        dma((5,)), dma((chunks,)), dma((chunks,)),
        dma((k_mp,)), dma((k_mp,)), dma((k_dp,)), dma((k_dp,)),
        dma((k_mp, chunks)), dma((k_mp, chunks)), dma((k_mp, chunks)), dma((k_mp, chunks)),
        dma((k_dp,)), dma((k_dp,)), dma((k_dp,)), dma((k_dp,)),
        dma((hops,)), dma((hops,)),
    ]
    anywhere = pl.BlockSpec(memory_space=pl.ANY)
    flops = 2 * rows * (depth_in * width_i + depth_out * width_o)
    flops += 2 * tokens * width_i * width_o * (1 + queries // QTOK)
    return pl.pallas_call(
        functools.partial(kernel, (n_mp, n_dp, chunks)),
        out_shape=(
            jax.ShapeDtypeStruct((width_i, width_o), F32),
            jax.ShapeDtypeStruct(small[1:], F32),
        ),
        in_specs=[anywhere] * 6,
        out_specs=(anywhere, pl.BlockSpec(memory_space=pltpu.VMEM)),
        scratch_shapes=scratch,
        cost_estimate=pl.CostEstimate(
            flops=flops,
            bytes_accessed=2 * depth_out * width_o + 4 * width_i * width_o,
            transcendentals=0,
        ),
        compiler_params=pltpu.CompilerParams(
            collective_id=0, has_side_effects=True, vmem_limit_bytes=63 * 2**20
        ),
    )(acts, query_acts, grads, query_grads, basis_in, basis_out)


def split_rows(joined, groups, first):
    width = joined.shape[1]
    shaped = joined.reshape(groups, joined.shape[0] // groups, width)
    return (shaped[:, :first].reshape(-1, width), shaped[:, first:].reshape(-1, width))


def plain(acts, grads, query_acts, query_grads, basis_in, basis_out):
    n_model = lax.axis_size("mp")
    n_data = lax.axis_size("dp")
    rows_in = jnp.concatenate([acts, query_acts], axis=0)
    rows_out = jnp.concatenate([grads, query_grads], axis=0)
    part_in = jnp.dot(
        lax.all_gather(rows_in, "mp", axis=0, tiled=True),
        basis_in,
        preferred_element_type=jnp.float32,
    )
    part_out = jnp.dot(
        lax.all_gather(rows_out, "dp", axis=0, tiled=True),
        basis_out,
        preferred_element_type=jnp.float32,
    )
    rot_in = lax.psum(part_in, "dp").astype(jnp.bfloat16)
    rot_out = lax.psum(part_out, "mp").astype(jnp.bfloat16)
    tok_in, qry_in = split_rows(rot_in, n_model, acts.shape[0])
    tok_out, qry_out = split_rows(rot_out, n_data, grads.shape[0])
    count = tok_in.shape[0]
    sq_in = (tok_in.astype(jnp.float32) ** 2).astype(jnp.bfloat16)
    sq_out = (tok_out.astype(jnp.float32) ** 2).astype(jnp.bfloat16)
    contract_rows = (((0,), (0,)), ((), ()))
    eigenvalues = (
        lax.dot_general(sq_in, sq_out, contract_rows, preferred_element_type=jnp.float32) / count
    )
    queries = qry_in.shape[0] // QTOK
    qa_blocks = qry_in.reshape(queries, QTOK, qry_in.shape[1])
    qg_blocks = qry_out.reshape(queries, QTOK, qry_out.shape[1])

    def one_query(carry, pair):
        left, right = pair
        rotated = (
            lax.dot_general(left, right, contract_rows, preferred_element_type=jnp.float32) / QTOK
        )
        precond = (rotated / (eigenvalues + 0.1)).astype(jnp.bfloat16)
        mapped = jnp.dot(tok_in, precond, preferred_element_type=jnp.float32)
        return (carry, jnp.sum(mapped * tok_out, axis=1))

    unused, partial_scores = lax.scan(one_query, jnp.zeros((), jnp.float32), (qa_blocks, qg_blocks))
    scores = lax.psum(partial_scores, ("dp", "mp")) * math.sqrt(QTOK / (basis_in.shape[1] * n_model * basis_out.shape[1] * n_data))
    return (eigenvalues, scores)


def shards(acts, grads, query_acts, query_grads, basis_in, basis_out):
    n_mp, n_dp = lax.axis_size("mp"), lax.axis_size("dp")
    width_i, width_o = basis_in.shape[1], basis_out.shape[1]
    chunks = 7
    owned = (acts.shape[0] + query_acts.shape[0]) * n_mp
    aligned = (
        n_mp == 2 ** log2(n_mp)
        and n_dp == 2 ** log2(n_dp)
        and k_fits(n_mp, n_dp)
        and width_o % (chunks * 256) == 0
        and width_i % 256 == 0
        and owned % (16 * n_mp) == 0
        and owned % (16 * n_dp) == 0
        and all(a.shape[0] % 16 == 0 for a in (acts, query_acts, grads, query_grads))
    )
    if aligned:
        return fused(
            n_mp, n_dp, chunks, acts, grads, query_acts, query_grads, basis_in, basis_out
        )
    return plain(acts, grads, query_acts, query_grads, basis_in, basis_out)


def k_fits(n_mp, n_dp):
    return n_dp > 1 and log2(n_mp) > log2(n_dp)


def solution(mesh):
    placed = (
        P("mp", "dp"),
        P("dp", "mp"),
        P("mp", "dp"),
        P("dp", "mp"),
        P("dp", "mp"),
        P("mp", "dp"),
    )
    return jax.shard_map(
        shards, mesh=mesh, in_specs=placed, out_specs=(P("mp", "dp"), P()), check_vma=False
    )
```

```python
import functools
import math

import jax
import jax.numpy as jnp
from jax import lax
from jax.experimental import pallas as pl
from jax.experimental.pallas import tpu as pltpu
from jax.sharding import PartitionSpec as P

QTOK = 16
F32 = jnp.float32
BF16 = jnp.bfloat16
MESH = pl.DeviceIdType.MESH


def bit(v, b):
    return (v // 2**b) % 2


def reverse_bits(v, k):
    return sum(bit(v, b) * 2 ** (k - 1 - b) for b in range(k))


def log2(n):
    return n.bit_length() - 1


def kernel(cfg, *refs):
    n_mp, n_dp, chunks = cfg
    k_mp, k_dp = log2(n_mp), log2(n_dp)
    (
        acts, q_acts, grads, q_grads, basis_in, basis_out, eig_out, scores_out,
        gin, gout, bin_v, bout_v, acc, send_rs, recv_rs, rot_out, acc_in, recv_in, rot_in,
        act_t, sq_act_t, qact_t, grad_t, sq_grad, qgrad, inverse, eig_v, part, part_in,
        load_sem, bout_sem, eig_sem, gin_s, gin_r, gout_s, gout_r,
        rs_s, rs_r, ag_s, ag_r, irs_s, irs_r, iag_s, iag_r, ps_s, ps_r,
    ) = refs
    dp, mp = lax.axis_index("dp"), lax.axis_index("mp")
    pos_m, pos_d = reverse_bits(mp, k_mp), reverse_bits(dp, k_dp)
    tok_m, qry_m = acts.shape[0], q_acts.shape[0]
    tok_d, qry_d = grads.shape[0], q_grads.shape[0]
    row_m, row_d = tok_m + qry_m, tok_d + qry_d
    rows = row_m * n_mp
    tokens, queries = tok_m * n_mp, qry_m * n_mp // QTOK
    width_i = basis_in.shape[1]
    cw = basis_out.shape[1] // chunks
    ti = 256

    def along_mp(b):
        return (dp, mp + (1 - 2 * bit(mp, b)) * 2**b)

    def along_dp(b):
        return (dp + (1 - 2 * bit(dp, b)) * 2**b, mp)

    def remote(src, dst, s, r, to):
        return pltpu.make_async_remote_copy(
            src_ref=src, dst_ref=dst, send_sem=s, recv_sem=r, device_id=to, device_id_type=MESH
        )

    def rows_at(start, size):
        return pl.ds(pl.multiple_of(start, 16), size)

    def split_start(me, k, step):
        size = rows // 2**step
        return sum(bit(me, b) * (rows // 2 ** (b + 1)) for b in range(step)), size

    barrier = pltpu.get_barrier_semaphore()
    for b in range(k_mp):
        pl.semaphore_signal(barrier, inc=1, device_id=along_mp(b), device_id_type=MESH)
    for b in range(k_dp):
        pl.semaphore_signal(barrier, inc=1, device_id=along_dp(b), device_id_type=MESH)

    def load_chunk(c):
        columns = pl.ds(pl.multiple_of(c * cw, 128), cw)
        return pltpu.make_async_copy(
            basis_out.at[:, columns], bout_v.at[lax.rem(c, 2)], bout_sem.at[c]
        )

    loads = [
        pltpu.make_async_copy(grads, gout.at[rows_at(pos_d * row_d, tok_d)], load_sem.at[0]),
        pltpu.make_async_copy(
            q_grads, gout.at[rows_at(pos_d * row_d + tok_d, qry_d)], load_sem.at[1]
        ),
        pltpu.make_async_copy(acts, gin.at[rows_at(pos_m * row_m, tok_m)], load_sem.at[2]),
        pltpu.make_async_copy(
            q_acts, gin.at[rows_at(pos_m * row_m + tok_m, qry_m)], load_sem.at[3]
        ),
    ]
    load_bin = pltpu.make_async_copy(basis_in, bin_v, load_sem.at[4])
    for copy in loads:
        copy.start()
    load_chunk(0).start()
    load_chunk(1).start()
    load_bin.start()
    pl.semaphore_wait(barrier, k_mp + k_dp)

    def gather_step(buf, me, pos, k, per, step, s, r, along):
        block = rows_at((pos // 2**step) * 2**step * per, per * 2**step)
        return remote(buf.at[block], buf.at[block], s.at[step], r.at[step], along(k - 1 - step))

    gin_steps = [
        gather_step(gin, mp, pos_m, k_mp, row_m, s, gin_s, gin_r, along_mp) for s in range(k_mp)
    ]
    gout_steps = [
        gather_step(gout, dp, pos_d, k_dp, row_d, s, gout_s, gout_r, along_dp) for s in range(k_dp)
    ]
    loads[0].wait()
    loads[1].wait()
    gout_steps[0].start()
    loads[2].wait()
    loads[3].wait()
    gin_steps[0].start()
    for s in range(1, k_mp):
        gin_steps[s - 1].wait_recv()
        gin_steps[s].start()
    for s in range(1, k_dp):
        gout_steps[s - 1].wait_recv()
        gout_steps[s].start()
    gout_steps[k_dp - 1].wait_recv()
    part[0] = jnp.zeros_like(part[0])

    rs_at, offset = [], 0
    for s in range(k_mp):
        rs_at.append(offset)
        offset += rows // 2 ** (s + 1)
    irs_at, offset = [], 0
    for s in range(k_dp):
        irs_at.append(offset)
        offset += rows // 2 ** (s + 1)

    def by_parity(c, even, odd):
        return even + (c % 2) * (odd - even)

    def bit_out(s, c):
        return by_parity(c, bit(mp, s), bit(mp, (s + 1) % k_mp))

    def peer_out(s, c):
        step = by_parity(c, 2**s, 2 ** ((s + 1) % k_mp))
        return (dp, mp + (1 - 2 * bit_out(s, c)) * step)

    def start_out(c, step):
        size = rows // 2**step
        return sum(bit_out(b, c) * (rows // 2 ** (b + 1)) for b in range(step)), size

    def rs_copy(s, c):
        size = rows // 2 ** (s + 1)
        slot = pl.ds(rs_at[s], size)
        return remote(
            send_rs.at[c, slot], recv_rs.at[c, slot], rs_s.at[s, c], rs_r.at[s, c], peer_out(s, c)
        )

    def ag_copy(s, c):
        start, size = start_out(c, k_mp - s)
        block = rows_at(start, size)
        return remote(
            rot_out.at[c, block], rot_out.at[c, block], ag_s.at[s, c], ag_r.at[s, c],
            peer_out(k_mp - 1 - s, c),
        )

    def irs_copy(s):
        start, size = split_start(dp, k_dp, s)
        half = size // 2
        src = rows_at(start + (1 - bit(dp, s)) * half, half)
        return remote(
            acc_in.at[src], recv_in.at[pl.ds(irs_at[s], half)], irs_s.at[s], irs_r.at[s], along_dp(s)
        )

    def iag_copy(s):
        start, size = split_start(dp, k_dp, k_dp - s)
        block = rows_at(start, size)
        return remote(
            rot_in.at[block], rot_in.at[block], iag_s.at[s], iag_r.at[s], along_dp(k_dp - 1 - s)
        )

    half = rows // 2

    def rotate_out(c):
        load_chunk(c).wait()
        slot, ring = lax.rem(c, 2), lax.rem(c, k_mp + 1)
        theirs = rows_at((1 - bit_out(0, c)) * half, half)
        mine = rows_at(bit_out(0, c) * half, half)
        tile = 256

        @pl.loop(0, cw // tile)
        def _(j):
            columns = pl.ds(pl.multiple_of(j * tile, tile), tile)
            out = jnp.dot(gout[theirs, :], bout_v[slot, :, columns], preferred_element_type=F32)
            send_rs[c, pl.ds(0, half), columns] = out.astype(BF16)

        rs_copy(0, c).start()

        @pl.loop(0, cw // tile)
        def _(j):
            columns = pl.ds(pl.multiple_of(j * tile, tile), tile)
            acc[ring, :, columns] = jnp.dot(
                gout[mine, :], bout_v[slot, :, columns], preferred_element_type=F32
            )

        @pl.when(c + 2 < chunks)
        def _():
            load_chunk(c + 2).start()

    def reduce_out(s, c):
        rs_copy(s - 1, c).wait_recv()
        ring = lax.rem(c, k_mp + 1)
        start, size = start_out(c, s)
        start = start - bit_out(0, c) * half
        if s == k_mp:
            total = acc[ring, rows_at(start, size), :] + recv_rs[
                c, pl.ds(rs_at[s - 1], size), :
            ].astype(F32)
            begin, _ = start_out(c, k_mp)
            rot_out[c, rows_at(begin, size), :] = total.astype(BF16)
            ag_copy(0, c).start()
            return
        part_size = size // 2
        theirs, mine = (1 - bit_out(s, c)) * part_size, bit_out(s, c) * part_size
        base = rs_at[s - 1]
        send_rs[c, pl.ds(rs_at[s], part_size), :] = (
            acc[ring, rows_at(start + theirs, part_size), :]
            + recv_rs[c, rows_at(base + theirs, part_size), :].astype(F32)
        ).astype(BF16)
        rs_copy(s, c).start()
        acc[ring, rows_at(start + mine, part_size), :] = acc[
            ring, rows_at(start + mine, part_size), :
        ] + recv_rs[c, rows_at(base + mine, part_size), :].astype(F32)

    def spread_out(s, c):
        ag_copy(s - 1, c).wait_recv()
        if s < k_mp:
            ag_copy(s, c).start()

    def rotate_in():
        gin_steps[k_mp - 1].wait_recv()
        load_bin.wait()

        @pl.loop(0, width_i // ti)
        def _(j):
            columns = pl.ds(pl.multiple_of(j * ti, ti), ti)
            acc_in[:, columns] = jnp.dot(
                gin[...], bin_v[:, columns], preferred_element_type=F32
            )

        irs_copy(0).start()

    def reduce_in(s):
        irs_copy(s - 1).wait_recv()
        start, size = split_start(dp, k_dp, s)
        where = rows_at(start, size)
        total = acc_in[where, :] + recv_in[pl.ds(irs_at[s - 1], size), :]
        if s == k_dp:
            rot_in[where, :] = total.astype(BF16)
            iag_copy(0).start()
        else:
            acc_in[where, :] = total
            irs_copy(s).start()

    def spread_in(s):
        iag_copy(s - 1).wait_recv()
        if s < k_dp:
            iag_copy(s).start()
            return
        order = [reverse_bits(m, k_mp) * row_m for m in range(n_mp)]
        for i in range(width_i // ti):
            cols = pl.ds(i * ti, ti)
            tok = jnp.concatenate([rot_in[pl.ds(p, tok_m), cols] for p in order], axis=0)
            qry = jnp.concatenate([rot_in[pl.ds(p + tok_m, qry_m), cols] for p in order], axis=0)
            flipped = tok.astype(F32).T
            act_t[cols, :] = flipped
            sq_act_t[cols, :] = (flipped * flipped).astype(BF16)
            qact_t[cols, :] = qry.astype(F32).T.astype(BF16)

    def eig_copy(c):
        columns = pl.ds(pl.multiple_of(c * cw, 128), cw)
        return pltpu.make_async_copy(
            eig_v.at[lax.rem(c, 2)], eig_out.at[:, columns], eig_sem.at[c]
        )

    def score(c):
        @pl.when(c >= 2)
        def _():
            eig_copy(c - 2).wait()

        order = [reverse_bits(d, k_dp) * row_d for d in range(n_dp)]
        for j in range(cw // ti):
            cols = pl.ds(j * ti, ti)
            tok = jnp.concatenate([rot_out[c, pl.ds(p, tok_d), cols] for p in order], axis=0)
            wide = tok.astype(F32)
            grad_t[cols, :] = wide.T.astype(BF16)
            sq_grad[:, cols] = (wide * wide).astype(BF16)
        for d, p in enumerate(order):
            qgrad[pl.ds(d * qry_d, qry_d), :] = rot_out[c, pl.ds(p + tok_d, qry_d), :]
        slot = lax.rem(c, 2)

        @pl.loop(0, width_i // ti)
        def _(i):
            at = pl.ds(pl.multiple_of(i * ti, ti), ti)
            eig = jnp.dot(sq_act_t[at, :], sq_grad[...], preferred_element_type=F32) * (
                1.0 / tokens
            )
            eig_v[slot, at, :] = eig
            inverse[at, :] = (1.0 / QTOK) / (eig + 0.1)

        eig_copy(c).start()

        tall = math.gcd(width_i, 512)
        group = math.gcd(queries, 2)

        @pl.loop(0, queries // group)
        def _(n):
            owner = lax.broadcasted_iota(jnp.int32, qgrad.shape, 0) // QTOK
            every = qgrad[...].astype(F32)
            rights = [
                jnp.where(owner == n * group + g, every, 0.0).astype(BF16) for g in range(group)
            ]
            totals = [jnp.zeros((1, tokens), F32)] * group
            for i in range(width_i // tall):
                at = pl.ds(i * tall, tall)
                for g in range(group):
                    rotated = jnp.dot(qact_t[at, :], rights[g], preferred_element_type=F32)
                    precond = (rotated * inverse[at, :]).astype(BF16)
                    mapped = jnp.dot(precond, grad_t[...], preferred_element_type=F32)
                    totals[g] = totals[g] + jnp.sum(mapped * act_t[at, :], axis=0, keepdims=True)
            for g in range(group):
                row = pl.ds(n * group + g, 1)
                part[0, row, :] = part[0, row, :] + totals[g]

    lag = 2 * k_mp

    @pl.loop(0, chunks + lag)
    def _(w):
        @pl.when(w < chunks)
        def _():
            rotate_out(w)

        def staged(s, run):
            @pl.when(jnp.logical_and(w >= s, w < chunks + s))
            def _():
                run(w - s)

        for s in range(1, k_mp + 1):
            staged(s, functools.partial(reduce_out, s))
        for s in range(1, k_mp):
            staged(k_mp + s, functools.partial(spread_out, s))

        in_stages = (
            [rotate_in]
            + [functools.partial(reduce_in, s) for s in range(1, k_dp + 1)]
            + [functools.partial(spread_in, s) for s in range(1, k_dp + 1)]
        )
        for n, run in enumerate(in_stages):
            pl.when(w == n + 1)(run)

        staged(lag, functools.partial(spread_out, k_mp))
        staged(lag, score)

    partners = [along_dp(b) for b in range(k_dp)] + [along_mp(b) for b in range(k_mp)]
    for n, to in enumerate(partners):
        copy = remote(part.at[n], part_in.at[n], ps_s.at[n], ps_r.at[n], to)
        copy.start()
        copy.wait_recv()
        part[n + 1] = part[n] + part_in[n]
        copy.wait_send()
    scale = math.sqrt(QTOK / (width_i * n_mp * basis_out.shape[1] * n_dp))
    scores_out[...] = part[len(partners)] * scale

    for copy in gin_steps + gout_steps:
        copy.wait_send()
    for s in range(k_dp):
        irs_copy(s).wait_send()
        iag_copy(s).wait_send()

    @pl.loop(0, chunks)
    def _(c):
        for s in range(k_mp):
            rs_copy(s, c).wait_send()
            ag_copy(s, c).wait_send()

    eig_copy(jnp.int32(chunks - 2)).wait()
    eig_copy(jnp.int32(chunks - 1)).wait()


def fused(n_mp, n_dp, chunks, acts, grads, query_acts, query_grads, basis_in, basis_out):
    k_mp, k_dp = log2(n_mp), log2(n_dp)
    rows = (acts.shape[0] + query_acts.shape[0]) * n_mp
    tokens = acts.shape[0] * n_mp
    queries = query_acts.shape[0] * n_mp
    depth_in, width_i = basis_in.shape
    depth_out, width_o = basis_out.shape
    cw = width_o // chunks
    moved = rows - rows // n_mp
    moved_in = rows - rows // n_dp
    hops = k_mp + k_dp
    small = (hops, queries // QTOK, tokens)
    dma = pltpu.SemaphoreType.DMA
    scratch = [
        pltpu.VMEM((rows, depth_in), BF16),
        pltpu.VMEM((rows, depth_out), BF16),
        pltpu.VMEM((depth_in, width_i), BF16),
        pltpu.VMEM((2, depth_out, cw), BF16),
        pltpu.VMEM((k_mp + 1, rows // 2, cw), F32),
        pltpu.VMEM((chunks, moved, cw), BF16),
        pltpu.VMEM((chunks, moved, cw), BF16),
        pltpu.VMEM((chunks, rows, cw), BF16),
        pltpu.VMEM((rows, width_i), F32),
        pltpu.VMEM((moved_in, width_i), F32),
        pltpu.VMEM((rows, width_i), BF16),
        pltpu.VMEM((width_i, tokens), F32),
        pltpu.VMEM((width_i, tokens), BF16),
        pltpu.VMEM((width_i, queries), BF16),
        pltpu.VMEM((cw, tokens), BF16),
        pltpu.VMEM((tokens, cw), BF16),
        pltpu.VMEM((queries, cw), BF16),
        pltpu.VMEM((width_i, cw), F32),
        pltpu.VMEM((2, width_i, cw), F32),
        pltpu.VMEM((hops + 1,) + small[1:], F32),
        pltpu.VMEM(small, F32),
        dma((5,)), dma((chunks,)), dma((chunks,)),
        dma((k_mp,)), dma((k_mp,)), dma((k_dp,)), dma((k_dp,)),
        dma((k_mp, chunks)), dma((k_mp, chunks)), dma((k_mp, chunks)), dma((k_mp, chunks)),
        dma((k_dp,)), dma((k_dp,)), dma((k_dp,)), dma((k_dp,)),
        dma((hops,)), dma((hops,)),
    ]
    anywhere = pl.BlockSpec(memory_space=pl.ANY)
    flops = 2 * rows * (depth_in * width_i + depth_out * width_o)
    flops += 2 * tokens * width_i * width_o * (1 + queries // QTOK)
    return pl.pallas_call(
        functools.partial(kernel, (n_mp, n_dp, chunks)),
        out_shape=(
            jax.ShapeDtypeStruct((width_i, width_o), F32),
            jax.ShapeDtypeStruct(small[1:], F32),
        ),
        in_specs=[anywhere] * 6,
        out_specs=(anywhere, pl.BlockSpec(memory_space=pltpu.VMEM)),
        scratch_shapes=scratch,
        cost_estimate=pl.CostEstimate(
            flops=flops,
            bytes_accessed=2 * depth_out * width_o + 4 * width_i * width_o,
            transcendentals=0,
        ),
        compiler_params=pltpu.CompilerParams(
            collective_id=0, has_side_effects=True, vmem_limit_bytes=63 * 2**20
        ),
    )(acts, query_acts, grads, query_grads, basis_in, basis_out)


def split_rows(joined, groups, first):
    width = joined.shape[1]
    shaped = joined.reshape(groups, joined.shape[0] // groups, width)
    return (shaped[:, :first].reshape(-1, width), shaped[:, first:].reshape(-1, width))


def plain(acts, grads, query_acts, query_grads, basis_in, basis_out):
    n_model = lax.axis_size("mp")
    n_data = lax.axis_size("dp")
    rows_in = jnp.concatenate([acts, query_acts], axis=0)
    rows_out = jnp.concatenate([grads, query_grads], axis=0)
    part_in = jnp.dot(
        lax.all_gather(rows_in, "mp", axis=0, tiled=True),
        basis_in,
        preferred_element_type=jnp.float32,
    )
    part_out = jnp.dot(
        lax.all_gather(rows_out, "dp", axis=0, tiled=True),
        basis_out,
        preferred_element_type=jnp.float32,
    )
    rot_in = lax.psum(part_in, "dp").astype(jnp.bfloat16)
    rot_out = lax.psum(part_out, "mp").astype(jnp.bfloat16)
    tok_in, qry_in = split_rows(rot_in, n_model, acts.shape[0])
    tok_out, qry_out = split_rows(rot_out, n_data, grads.shape[0])
    count = tok_in.shape[0]
    sq_in = (tok_in.astype(jnp.float32) ** 2).astype(jnp.bfloat16)
    sq_out = (tok_out.astype(jnp.float32) ** 2).astype(jnp.bfloat16)
    contract_rows = (((0,), (0,)), ((), ()))
    eigenvalues = (
        lax.dot_general(sq_in, sq_out, contract_rows, preferred_element_type=jnp.float32) / count
    )
    queries = qry_in.shape[0] // QTOK
    qa_blocks = qry_in.reshape(queries, QTOK, qry_in.shape[1])
    qg_blocks = qry_out.reshape(queries, QTOK, qry_out.shape[1])

    def one_query(carry, pair):
        left, right = pair
        rotated = (
            lax.dot_general(left, right, contract_rows, preferred_element_type=jnp.float32) / QTOK
        )
        precond = (rotated / (eigenvalues + 0.1)).astype(jnp.bfloat16)
        mapped = jnp.dot(tok_in, precond, preferred_element_type=jnp.float32)
        return (carry, jnp.sum(mapped * tok_out, axis=1))

    unused, partial_scores = lax.scan(one_query, jnp.zeros((), jnp.float32), (qa_blocks, qg_blocks))
    scores = lax.psum(partial_scores, ("dp", "mp")) * math.sqrt(QTOK / (basis_in.shape[1] * n_model * basis_out.shape[1] * n_data))
    return (eigenvalues, scores)


def shards(acts, grads, query_acts, query_grads, basis_in, basis_out):
    n_mp, n_dp = lax.axis_size("mp"), lax.axis_size("dp")
    width_i, width_o = basis_in.shape[1], basis_out.shape[1]
    chunks = 7
    owned = (acts.shape[0] + query_acts.shape[0]) * n_mp
    aligned = (
        n_mp == 2 ** log2(n_mp)
        and n_dp == 2 ** log2(n_dp)
        and k_fits(n_mp, n_dp)
        and width_o % (chunks * 256) == 0
        and width_i % 256 == 0
        and owned % (16 * n_mp) == 0
        and owned % (16 * n_dp) == 0
        and all(a.shape[0] % 16 == 0 for a in (acts, query_acts, grads, query_grads))
    )
    if aligned:
        return fused(
            n_mp, n_dp, chunks, acts, grads, query_acts, query_grads, basis_in, basis_out
        )
    return plain(acts, grads, query_acts, query_grads, basis_in, basis_out)


def k_fits(n_mp, n_dp):
    return n_dp > 1 and log2(n_mp) > log2(n_dp)


def solution(mesh):
    placed = (
        P("mp", "dp"),
        P("dp", "mp"),
        P("mp", "dp"),
        P("dp", "mp"),
        P("dp", "mp"),
        P("mp", "dp"),
    )
    return jax.shard_map(
        shards, mesh=mesh, in_specs=placed, out_specs=(P("mp", "dp"), P()), check_vma=False
    )
```
